32 devices in a mesh: cube: 8 (over z, y), pair: 4 (over x, core).
Axes of the slice: x: 2, y: 2, z: 4, core: 2. Of those that a mesh axis runs over, the one named last changes fastest.
Arguments:
- own_partial: float32 [3, 2048, 512], P(None, 'cube'), may hold values from -6 to 6
- spill_partial: float32 [3, 2048, 512], P(None, 'cube'), may hold values from -6 to 6
- spill_box: int32 [2048], P('cube'), may hold values from 0 to 255, as said below
- sources: int32 [2048, 189], P('cube'), may hold values from 0 to 2047, as said below
- reflections: int32 [2048, 189], P('cube'), may hold values from 0 to 15
- operators: bfloat16 [16, 512, 512], P('pair'), may hold values from -0.01953125 to 0.01953125
Outputs:
- local_own: float32 [3, 2048, 512], P(None, 'cube', 'pair')
- local_spill: float32 [3, 2048, 512], P(None, 'cube', 'pair')
The draws below stay inside these ranges and needn't reach their ends.
Inputs may be any that keep to these rules, and one draw needn't show every extreme that they name: The sources of box b lie on b's owner or on the owner just before or after it: from max(0, (b // 256 - 1) * 256) to min(2048, (b // 256 + 2) * 256) - 1. A source may repeat within a list. `spill_box`: the 64 entries of each aligned run of 64 are distinct.
All inputs are finite; a program needn't handle non-finite values.
Results may differ from the reference program's by a relative error of at most 0.0095.
Values may be sent and summed in bfloat16 or wider, within the bound.
A program may use at most 64 MiB of HBM per device.

```python
import jax
import jax.numpy as jnp
from jax import lax

E = 512
LIST = 189
REFL = 16
SPILL = 2
BOX_DEV = 256
CAPS = 64
SPILL_SLOTS = 256
SPILL_ALL = 2048
BOXES = 2048


def draw_spill_box(key, part):
    run_count = SPILL_ALL // CAPS
    scores = jax.random.randint(key, (run_count, BOX_DEV), 0, 1 << 20, dtype=jnp.int32)
    scores = scores * BOX_DEV + jnp.arange(BOX_DEV, dtype=jnp.int32)[None, :]
    ordering = jnp.argsort(scores, axis=1)
    return ordering[:, :CAPS].reshape(SPILL_ALL).astype(jnp.int32)


def draw_sources(key, part):
    owner_ids = jnp.arange(BOXES, dtype=jnp.int32) // BOX_DEV
    lowest = jnp.maximum(0, (owner_ids - 1) * BOX_DEV)
    highest = jnp.minimum(BOXES, (owner_ids + 2) * BOX_DEV)
    return jax.random.randint(key, (BOXES, LIST), lowest[:, None], highest[:, None], dtype=jnp.int32)


def set_ends(drawn, rng, least, largest):
    shape = drawn.shape
    place = [jax.random.randint(jax.random.fold_in(rng, axis), (), 0, shape[axis]) for axis in range(len(shape))]
    drawn = drawn.at[tuple(place)].set(least)
    longest = shape.index(max(shape))
    place[longest] = (place[longest] + 1) % shape[longest]
    return drawn.at[tuple(place)].set(largest)


def levels(rng, extent, pieces, least, high):
    loudness, own = 1.0, jax.random.fold_in(rng, 6)
    for position, blocks in pieces:
        steps = jnp.exp(jax.random.uniform(jax.random.fold_in(own, position), (blocks,), jnp.float32, least / len(pieces), high / len(pieces)))
        loudness = loudness * jnp.repeat(steps, extent[position] // blocks).reshape([-1 if axis == position else 1 for axis in range(len(extent))])
    return loudness


def bell_draw(own_key, extent, scale, most, cuts=(), kind=jnp.bfloat16):
    result = scale * jax.random.normal(own_key, extent, jnp.float32)
    if cuts:
        result = result * levels(own_key, extent, cuts, -0.22, 0.18)
    return jnp.clip(result, -most, most).astype(kind)


def setup_inputs(seed: int = 0) -> dict:
    streams_of = jax.random.split(jax.random.key(seed), 7)
    return {
        "own_partial": bell_draw(streams_of[0], (3, BOXES, E), 1.0, 6.0, ((1, 8),), jnp.float32),
        "spill_partial": bell_draw(streams_of[1], (3, SPILL_ALL, E), 1.0, 6.0, ((1, 8),), jnp.float32),
        "spill_box": draw_spill_box(jax.random.fold_in(streams_of[6], 71), 0),
        "sources": draw_sources(jax.random.fold_in(streams_of[6], 71), 0),
        "reflections": set_ends(jax.random.randint(streams_of[4], (BOXES, LIST), 0, REFL), jax.random.fold_in(streams_of[4], 1), 0, REFL - 1).astype(jnp.int32),
        "operators": bell_draw(streams_of[5], (REFL, E, E), (E * LIST) ** -0.5, 0.01953125, ((0, 4),)),
    }


def slot_targets():
    owner_count = BOXES // BOX_DEV
    slot_ids = jnp.arange(SPILL_ALL, dtype=jnp.int32)
    device_ids = slot_ids // SPILL_SLOTS
    group_ids = (slot_ids % SPILL_SLOTS) // CAPS
    offsets = jnp.where(group_ids < SPILL, group_ids - SPILL, group_ids - SPILL + 1)
    owners = device_ids + offsets
    valid = (owners >= 0) & (owners < owner_count)
    return owners, valid


def reference(own_partial, spill_partial, spill_box, sources, reflections, operators):
    owners, valid = slot_targets()
    slot_box = jnp.where(valid, owners * BOX_DEV + spill_box, BOXES).astype(jnp.int32)
    spill_rows = jnp.moveaxis(spill_partial, 1, 0)
    added = jax.ops.segment_sum(spill_rows, slot_box, num_segments=BOXES + 1)[:BOXES]
    multipole = (own_partial + jnp.moveaxis(added, 0, 1)).astype(jnp.bfloat16)
    refl_ids = jnp.arange(REFL, dtype=jnp.int32)[:, None]
    comp_ids = jnp.arange(3, dtype=jnp.int32)[None, :]
    sign_table = (1 - 2 * (jnp.right_shift(refl_ids, comp_ids) & 1)).astype(jnp.float32)
    transformed = jnp.einsum("cbe,ref->rcbf", multipole.astype(jnp.float32), operators.astype(jnp.float32),
                             precision=lax.Precision.HIGHEST)
    transformed = transformed * sign_table[:, :, None, None]
    blocks = BOXES // BOX_DEV
    src_blocks = sources.reshape(blocks, BOX_DEV, LIST)
    refl_blocks = reflections.reshape(blocks, BOX_DEV, LIST)

    def one_block(pair_in):
        src_part, refl_part = pair_in
        picked = transformed[refl_part, :, src_part, :]
        return jnp.sum(picked, axis=1)

    summed = lax.map(one_block, (src_blocks, refl_blocks))
    local_own = jnp.moveaxis(summed.reshape(BOXES, 3, E), 0, 1)
    safe_box = jnp.minimum(slot_box, BOXES - 1).astype(jnp.int32)
    local_spill = jnp.where(valid[None, :, None], local_own[:, safe_box, :], jnp.float32(0.0))
    return local_own, local_spill
```

```python
import functools

import jax
import jax.numpy as jnp
from jax import lax
from jax.experimental import pallas as pl
from jax.experimental.pallas import tpu as pltpu
from jax.sharding import PartitionSpec as P

SPILL = 2
LOW, OWN, HIGH = 0, 1, 2
LANES = 128
BF = jnp.bfloat16
F32 = jnp.float32


def shifts():
    return [k for k in range(-SPILL, SPILL + 1) if k != 0]


def kernel(
    cubes, pairs,
    own_hbm, spill_hbm, box_ref, src_ref, refl_ref, op_hbm,
    own_out, spill_out,
    own_v, spill_v, op_v, lab_send, lab_recv, sp_send, sp_recv,
    key_hi, key_lo, cnt_f, cnt, win, mixed, part, rs1_send, rs1_recv, rs2_send, rs2_recv,
    field, rt_send, rt_recv,
    local_sem, lab_sem, sp_sem, halo_sem, far_sem, near_sem, rs1_sem, rs2_sem, rt_sem,
):
    c = lax.axis_index("cube")
    p = lax.axis_index("pair")
    half = pairs // 2
    far = lax.rem(p + half, pairs)
    near = p + 1 - 2 * lax.rem(p, 2)
    hi, lo = p // 2, lax.rem(p, 2)
    comps, boxes, q = own_v.shape
    held, coeffs, outs = op_v.shape
    slots = sp_send.shape[1]
    extent = 3 * boxes
    tiles = extent // LANES
    rows = cnt_f.shape[0] // boxes
    entries = src_ref.shape[1]

    def inside(k):
        return (c + k >= 0) & (c + k < cubes)

    def remote(src, dst, sems, **where):
        return pltpu.make_async_remote_copy(
            src_ref=src, dst_ref=dst, send_sem=sems.at[0], recv_sem=sems.at[1],
            device_id=where, device_id_type=pl.DeviceIdType.MESH,
        )

    barrier = pltpu.get_barrier_semaphore()
    partners = 2
    for other in (far, near):
        pl.semaphore_signal(barrier, inc=1, device_id={"pair": other}, device_id_type=pl.DeviceIdType.MESH)
    for k in shifts():
        partners = partners + inside(k).astype(jnp.int32)

        @pl.when(inside(k))
        def _():
            pl.semaphore_signal(barrier, inc=1, device_id={"cube": c + k}, device_id_type=pl.DeviceIdType.MESH)

    mine = pl.ds(pl.multiple_of(p * q, q), q)
    read_spill = pltpu.make_async_copy(spill_hbm.at[:, :, mine], spill_v, local_sem.at[0])
    read_own = pltpu.make_async_copy(own_hbm.at[:, :, mine], own_v, local_sem.at[1])
    read_op = pltpu.make_async_copy(op_hbm, op_v, local_sem.at[2])
    read_spill.start()
    read_own.start()
    read_op.start()

    groups = list(enumerate(shifts()))
    for g, k in groups:
        lab_send[g, 0:1, 0:slots] = box_ref[0:1, g * slots:(g + 1) * slots]
    read_spill.wait()
    for g, k in groups:
        for m in range(comps):
            sp_send[g, :, m * q:(m + 1) * q] = spill_v[m, g * slots:(g + 1) * slots, :].astype(BF)
    pl.semaphore_wait(barrier, partners)

    def send_spill(g, k):
        return remote(sp_send.at[g], sp_recv.at[g], sp_sem.at[g], cube=c + k)

    def send_label(g, k):
        return remote(lab_send.at[g], lab_recv.at[g], lab_sem.at[g], cube=c + k)

    for g, k in groups:
        @pl.when(inside(k))
        def _(g=g, k=k):
            send_spill(g, k).start()
            send_label(g, k).start()

    rel = refl_ref[...] - p * held
    ok = (rel >= 0) & (rel < held)
    key = rel * extent + src_ref[...] - (c - 1) * boxes
    key_hi[...] = jnp.full(key_hi.shape, -1.0, F32)
    key_lo[...] = jnp.zeros(key_lo.shape, F32)
    key_hi[:, 0:entries] = jnp.where(ok, lax.shift_right_arithmetic(key, 7), -1).astype(F32)
    key_lo[:, 0:entries] = jnp.where(ok, key & (LANES - 1), 0).astype(F32)

    width = key_hi.shape[1]
    ids_hi = lax.broadcasted_iota(jnp.int32, (rows, width), 0).astype(F32).astype(BF)
    ids_lo = lax.broadcasted_iota(jnp.int32, (LANES, width), 0).astype(F32).astype(BF)
    one, zero = jnp.ones((), BF), jnp.zeros((), BF)

    def count(step, carry):
        base = pl.multiple_of(step * 8, 8)
        his = key_hi[pl.ds(base, 8), :]
        los = key_lo[pl.ds(base, 8), :]
        for u in range(8):
            a = jnp.where(his[u:u + 1].astype(BF) == ids_hi, one, zero)
            b = jnp.where(los[u:u + 1].astype(BF) == ids_lo, one, zero)
            got = lax.dot_general(a, b, (((1,), (1,)), ((), ())), preferred_element_type=F32)
            cnt_f[pl.ds(pl.multiple_of((base + u) * rows, rows), rows), :] = got
        return carry

    steps = boxes // 8
    lax.fori_loop(0, steps // 2, count, 0)

    read_own.wait()
    box_ids = lax.broadcasted_iota(jnp.int32, (boxes, slots), 0)

    def picker(g):
        return jnp.where(lab_recv[g, 0:1, 0:slots] == box_ids, 1.0, 0.0).astype(BF)

    for g, k in groups:
        @pl.when(inside(-k))
        def _(g=g, k=k):
            send_spill(g, k).wait_recv()
            send_label(g, k).wait_recv()
            more = jnp.dot(picker(g), sp_recv[g], preferred_element_type=F32)
            for m in range(comps):
                own_v[m] += more[:, m * q:(m + 1) * q]

    for m in range(comps):
        win[p, OWN, m] = own_v[m].astype(BF)

    def up(m):
        return remote(win.at[p, OWN, m], win.at[p, LOW, m], halo_sem.at[0, m], cube=c + 1)

    def down(m):
        return remote(win.at[p, OWN, m], win.at[p, HIGH, m], halo_sem.at[1, m], cube=c - 1)

    def to_far(b, m):
        return remote(win.at[p, b, m], win.at[p, b, m], far_sem.at[b, m], pair=far)

    def to_near(b, m, which):
        owner = (p, far)[which]
        return remote(win.at[owner, b, m], win.at[owner, b, m], near_sem.at[which, b, m], pair=near)

    for m in range(comps):
        @pl.when(inside(1))
        def _():
            up(m).start()

        @pl.when(inside(-1))
        def _():
            down(m).start()

        to_far(OWN, m).start()
        to_near(OWN, m, 0).start()

    @pl.when(jnp.logical_not(inside(-1)))
    def _():
        win[p, LOW] = jnp.zeros(win.shape[2:], BF)

    @pl.when(jnp.logical_not(inside(1)))
    def _():
        win[p, HIGH] = jnp.zeros(win.shape[2:], BF)

    lax.fori_loop(steps // 2, steps, count, 0)

    def relay(m):
        @pl.when(inside(-1))
        def _():
            up(m).wait_recv()

        to_far(LOW, m).start()
        to_near(LOW, m, 0).start()

        @pl.when(inside(1))
        def _():
            down(m).wait_recv()

        to_far(HIGH, m).start()
        to_near(HIGH, m, 0).start()
        to_far(OWN, m).wait_recv()
        to_near(OWN, m, 1).start()

    def pass_near(m):
        for b in (LOW, HIGH):
            to_far(b, m).wait_recv()
            to_near(b, m, 1).start()

    def reduce_near(m):
        return remote(rs1_send.at[m], rs1_recv.at[m], rs1_sem.at[m], pair=near)

    def reduce_far(m):
        return remote(rs2_send.at[m], rs2_recv.at[m], rs2_sem.at[m], pair=far)

    def columns(index):
        return pl.ds(pl.multiple_of(index * q, q), q)

    def compute(m):
        for b in (LOW, OWN, HIGH):
            for which in range(2):
                to_near(b, m, which).wait_recv()
        window = jnp.concatenate(
            [jnp.concatenate([win[s, b, m] for s in range(pairs)], axis=1) for b in (LOW, OWN, HIGH)],
            axis=0,
        )
        for r in range(held):
            sign = 1 - 2 * (lax.shift_right_logical(p * held + r, m) & 1)
            summed = jnp.dot(cnt[r * boxes:(r + 1) * boxes, :], window, preferred_element_type=F32)
            mixed[:, r * coeffs:(r + 1) * coeffs] = (summed * sign.astype(F32)).astype(BF)
        part[m] = jnp.dot(
            mixed[...], op_v[...].reshape(held * coeffs, outs), preferred_element_type=F32
        )
        for h in range(half):
            rs1_send[m, h] = part[m, :, columns(2 * h + 1 - lo)].astype(BF)
        reduce_near(m).start()

    def fold(m):
        reduce_near(m).wait_recv()
        there = far // 2
        rs2_send[m] = (part[m, :, columns(far)] + rs1_recv[m, there].astype(F32)).astype(BF)
        reduce_far(m).start()

    def finish(m):
        reduce_far(m).wait_recv()
        total = part[m, :, columns(p)] + rs1_recv[m, hi].astype(F32) + rs2_recv[m].astype(F32)
        own_out[m] = total
        field[:, m * q:(m + 1) * q] = total.astype(BF)

    relay(0)
    for r in range(held):
        for t in range(tiles):
            cnt[r * boxes:(r + 1) * boxes, t * LANES:(t + 1) * LANES] = cnt_f[
                pl.ds(r * tiles + t, boxes, stride=rows), :
            ].astype(BF)
    relay(1)
    pass_near(0)
    relay(2)
    pass_near(1)
    read_op.wait()
    compute(0)
    pass_near(2)
    compute(1)
    fold(0)
    compute(2)
    fold(1)
    finish(0)
    fold(2)
    finish(1)
    finish(2)

    def send_back(g, k):
        return remote(rt_send.at[g], rt_recv.at[g], rt_sem.at[g], cube=c - k)

    for g, k in groups:
        @pl.when(inside(-k))
        def _(g=g, k=k):
            rt_send[g] = lax.dot_general(
                picker(g), field[...], (((0,), (0,)), ((), ())), preferred_element_type=F32
            ).astype(BF)
            send_back(g, k).start()

    for g, k in groups:
        rows_out = slice(g * slots, (g + 1) * slots)

        @pl.when(inside(k))
        def _(g=g, k=k, rows_out=rows_out):
            send_back(g, k).wait_recv()
            for m in range(comps):
                spill_out[m, rows_out, :] = rt_recv[g, :, m * q:(m + 1) * q].astype(F32)

        @pl.when(jnp.logical_not(inside(k)))
        def _(rows_out=rows_out):
            for m in range(comps):
                spill_out[m, rows_out, :] = jnp.zeros((slots, q), F32)

    for g, k in groups:
        @pl.when(inside(k))
        def _(g=g, k=k):
            send_spill(g, k).wait_send()
            send_label(g, k).wait_send()

        @pl.when(inside(-k))
        def _(g=g, k=k):
            send_back(g, k).wait_send()

    for m in range(comps):
        @pl.when(inside(1))
        def _(m=m):
            up(m).wait_send()

        @pl.when(inside(-1))
        def _(m=m):
            down(m).wait_send()

        for b in (LOW, OWN, HIGH):
            to_far(b, m).wait_send()
            to_near(b, m, 0).wait_send()
            to_near(b, m, 1).wait_send()
        reduce_near(m).wait_send()
        reduce_far(m).wait_send()


def on_device(cubes, pairs, own_partial, spill_partial, spill_box, sources, reflections, operators):
    comps, boxes, coeffs = own_partial.shape
    held, _, outs = operators.shape
    spills = spill_box.shape[0]
    groups = 2 * SPILL
    slots = spills // groups
    q = coeffs // pairs
    extent = 3 * boxes
    rows = -(-(held * extent // LANES) // 16) * 16
    width = -(-sources.shape[1] // LANES) * LANES
    dma = pltpu.SemaphoreType.DMA
    vmem = pl.BlockSpec(memory_space=pltpu.VMEM)
    anywhere = pl.BlockSpec(memory_space=pl.ANY)
    return pl.pallas_call(
        functools.partial(kernel, cubes, pairs),
        out_shape=(
            jax.ShapeDtypeStruct((comps, boxes, q), F32),
            jax.ShapeDtypeStruct((comps, spills, q), F32),
        ),
        in_specs=[anywhere, anywhere, vmem, vmem, vmem, anywhere],
        out_specs=(vmem, vmem),
        scratch_shapes=[
            pltpu.VMEM((comps, boxes, q), F32),
            pltpu.VMEM((comps, spills, q), F32),
            pltpu.VMEM((held, coeffs, outs), BF),
            pltpu.VMEM((groups, 8, LANES), jnp.int32),
            pltpu.VMEM((groups, 8, LANES), jnp.int32),
            pltpu.VMEM((groups, slots, comps * q), BF),
            pltpu.VMEM((groups, slots, comps * q), BF),
            pltpu.VMEM((boxes, width), F32),
            pltpu.VMEM((boxes, width), F32),
            pltpu.VMEM((boxes * rows, LANES), F32),
            pltpu.VMEM((held * boxes, extent), BF),
            pltpu.VMEM((pairs, 3, comps, boxes, q), BF),
            pltpu.VMEM((boxes, held * coeffs), BF),
            pltpu.VMEM((comps, boxes, outs), F32),
            pltpu.VMEM((comps, pairs // 2, boxes, q), BF),
            pltpu.VMEM((comps, pairs // 2, boxes, q), BF),
            pltpu.VMEM((comps, boxes, q), BF),
            pltpu.VMEM((comps, boxes, q), BF),
            pltpu.VMEM((boxes, comps * q), BF),
            pltpu.VMEM((groups, slots, comps * q), BF),
            pltpu.VMEM((groups, slots, comps * q), BF),
            dma((3,)),
            dma((groups, 2)),
            dma((groups, 2)),
            dma((2, comps, 2)),
            dma((3, comps, 2)),
            dma((2, 3, comps, 2)),
            dma((comps, 2)),
            dma((comps, 2)),
            dma((groups, 2)),
        ],
        compiler_params=pltpu.CompilerParams(
            collective_id=0, has_side_effects=True, vmem_limit_bytes=40 * 1024 * 1024
        ),
        name="far_field",
    )(own_partial, spill_partial, spill_box.reshape(1, spills), sources, reflections, operators)


def solution(mesh):
    cubes, pairs = mesh.shape["cube"], mesh.shape["pair"]
    in_specs = (
        P(None, "cube", None),
        P(None, "cube", None),
        P("cube"),
        P("cube", None),
        P("cube", None),
        P("pair", None, None),
    )
    out_specs = (P(None, "cube", "pair"), P(None, "cube", "pair"))
    return jax.shard_map(
        functools.partial(on_device, cubes, pairs),
        mesh=mesh, in_specs=in_specs, out_specs=out_specs, check_vma=False,
    )
```

```python
import functools

import jax
import jax.numpy as jnp
from jax import lax
from jax.experimental import pallas as pl
from jax.experimental.pallas import tpu as pltpu
from jax.sharding import PartitionSpec as P

SPILL = 2
LOW, OWN, HIGH = 0, 1, 2
LANES = 128
COUNT_CUTS = (0, 4, 8, 12, 16, 16)
BF = jnp.bfloat16
F32 = jnp.float32


def shifts():
    return [k for k in range(-SPILL, SPILL + 1) if k != 0]


def kernel(
    cubes, pairs,
    own_hbm, spill_hbm, box_hbm, src_hbm, refl_hbm, op_hbm,
    own_out, spill_out,
    own_v, spill_v, op_v, box_ref, src_ref, refl_ref, lab_send, lab_recv, sp_send, sp_recv,
    keys, key_hi, key_lo, cnt_f, cnt, win, mixed, part, rs1_send, rs1_recv, rs2_send, rs2_recv,
    pick, pick_t, rt_send, rt_recv,
    local_sem, lab_sem, sp_sem, halo_sem, far_sem, near_sem, rs1_sem, rs2_sem, rt_sem,
):
    c = lax.axis_index("cube")
    p = lax.axis_index("pair")
    half = pairs // 2
    far = lax.rem(p + half, pairs)
    near = p + 1 - 2 * lax.rem(p, 2)
    hi, lo = p // 2, lax.rem(p, 2)
    comps, boxes, q = own_v.shape
    held, coeffs, outs = op_v.shape
    slots = sp_send.shape[2]
    extent = 3 * boxes
    tiles = extent // LANES
    rows = cnt_f.shape[0] // boxes
    entries = src_ref.shape[0]

    def inside(k):
        return (c + k >= 0) & (c + k < cubes)

    def remote(src, dst, sems, **where):
        return pltpu.make_async_remote_copy(
            src_ref=src, dst_ref=dst, send_sem=sems.at[0], recv_sem=sems.at[1],
            device_id=where, device_id_type=pl.DeviceIdType.MESH,
        )

    barrier = pltpu.get_barrier_semaphore()
    partners = 2
    for other in (far, near):
        pl.semaphore_signal(barrier, inc=1, device_id={"pair": other}, device_id_type=pl.DeviceIdType.MESH)
    for k in shifts():
        partners = partners + inside(k).astype(jnp.int32)

        @pl.when(inside(k))
        def _():
            pl.semaphore_signal(barrier, inc=1, device_id={"cube": c + k}, device_id_type=pl.DeviceIdType.MESH)

    mine = pl.ds(pl.multiple_of(p * q, q), q)
    read_spill = pltpu.make_async_copy(spill_hbm.at[:, :, mine], spill_v, local_sem.at[0])
    read_own = pltpu.make_async_copy(own_hbm.at[:, :, mine], own_v, local_sem.at[1])
    read_op = pltpu.make_async_copy(op_hbm, op_v, local_sem.at[2])
    read_box = pltpu.make_async_copy(box_hbm, box_ref, local_sem.at[3])
    read_src = pltpu.make_async_copy(src_hbm, src_ref, local_sem.at[4])
    read_refl = pltpu.make_async_copy(refl_hbm, refl_ref, local_sem.at[5])
    read_box.start()
    read_spill.start()
    read_src.start()
    read_refl.start()
    read_own.start()
    read_op.start()

    groups = list(enumerate(shifts()))

    def send_spill(g, k, m):
        return remote(sp_send.at[g, m], sp_recv.at[g, m], sp_sem.at[g, m], cube=c + k)

    def send_label(g, k):
        return remote(lab_send.at[g], lab_recv.at[g], lab_sem.at[g], cube=c + k)

    read_box.wait()
    for g, k in groups:
        lab_send[g, 0:1, 0:slots] = box_ref[0:1, g * slots:(g + 1) * slots]
    read_spill.wait()
    for m in range(comps):
        for g, k in groups:
            sp_send[g, m] = spill_v[m, g * slots:(g + 1) * slots, :].astype(BF)
        if m == 0:
            pl.semaphore_wait(barrier, partners)
            for g, k in groups:
                @pl.when(inside(k))
                def _(g=g, k=k):
                    send_label(g, k).start()

        for g, k in groups:
            @pl.when(inside(k))
            def _(g=g, k=k, m=m):
                send_spill(g, k, m).start()

    read_src.wait()
    read_refl.wait()
    rel = refl_ref[...] - p * held
    ok = (rel >= 0) & (rel < held)
    key = rel * extent + src_ref[...] - (c - 1) * boxes
    keys[...] = jnp.full(keys.shape, -1.0, F32)
    keys[0:entries, :] = jnp.where(ok, key, -1).astype(F32)
    turned = jnp.transpose(keys[...]).astype(jnp.int32)
    key_hi[...] = lax.shift_right_arithmetic(turned, 7).astype(F32)
    key_lo[...] = (turned & (LANES - 1)).astype(F32)

    width = key_hi.shape[1]
    ids_hi = lax.broadcasted_iota(jnp.int32, (rows, width), 0).astype(F32).astype(BF)
    ids_lo = lax.broadcasted_iota(jnp.int32, (LANES, width), 0).astype(F32).astype(BF)
    one, zero = jnp.ones((), BF), jnp.zeros((), BF)

    def count(step, carry):
        base = pl.multiple_of(step * 16, 16)
        his = key_hi[pl.ds(base, 16), :]
        los = key_lo[pl.ds(base, 16), :]
        for u in range(16):
            a = jnp.where(his[u:u + 1].astype(BF) == ids_hi, one, zero)
            b = jnp.where(los[u:u + 1].astype(BF) == ids_lo, one, zero)
            got = lax.dot_general(a, b, (((1,), (1,)), ((), ())), preferred_element_type=F32)
            cnt_f[pl.ds(pl.multiple_of((base + u) * rows, rows), rows), :] = got
        return carry

    steps = boxes // 16
    cuts = [steps * part_of // 16 for part_of in COUNT_CUTS]

    def count_part(i):
        lax.fori_loop(cuts[i], cuts[i + 1], count, 0)

    count_part(0)

    read_own.wait()
    box_ids = lax.broadcasted_iota(jnp.int32, (boxes, slots), 0)

    for g, k in groups:
        @pl.when(inside(-k))
        def _(g=g, k=k):
            send_label(g, k).wait_recv()
            pick[g] = jnp.where(lab_recv[g, 0:1, 0:slots] == box_ids, 1.0, 0.0).astype(BF)

        @pl.when(jnp.logical_not(inside(-k)))
        def _(g=g):
            pick[g] = jnp.zeros((boxes, slots), BF)

    def up(m):
        return remote(win.at[p, OWN, m], win.at[p, LOW, m], halo_sem.at[0, m], cube=c + 1)

    def down(m):
        return remote(win.at[p, OWN, m], win.at[p, HIGH, m], halo_sem.at[1, m], cube=c - 1)

    def to_far(b, m):
        return remote(win.at[p, b, m], win.at[p, b, m], far_sem.at[b, m], pair=far)

    def to_near(b, m, which):
        owner = (p, far)[which]
        return remote(win.at[owner, b, m], win.at[owner, b, m], near_sem.at[which, b, m], pair=near)

    for m in range(comps):
        for g, k in groups:
            @pl.when(inside(-k))
            def _(g=g, k=k, m=m):
                send_spill(g, k, m).wait_recv()
                own_v[m] += jnp.dot(pick[g], sp_recv[g, m], preferred_element_type=F32)

        win[p, OWN, m] = own_v[m].astype(BF)

        @pl.when(inside(1))
        def _(m=m):
            up(m).start()

        @pl.when(inside(-1))
        def _(m=m):
            down(m).start()

        if m < comps - 1:
            to_far(OWN, m).start()
        to_near(OWN, m, 0).start()

    @pl.when(jnp.logical_not(inside(-1)))
    def _():
        win[p, LOW] = jnp.zeros(win.shape[2:], BF)

    @pl.when(jnp.logical_not(inside(1)))
    def _():
        win[p, HIGH] = jnp.zeros(win.shape[2:], BF)

    count_part(1)

    def relay(m):
        @pl.when(inside(-1))
        def _():
            up(m).wait_recv()

        to_far(LOW, m).start()
        to_near(LOW, m, 0).start()

        @pl.when(inside(1))
        def _():
            down(m).wait_recv()

        to_far(HIGH, m).start()
        to_near(HIGH, m, 0).start()
        if m < comps - 1:
            to_far(OWN, m).wait_recv()
            to_near(OWN, m, 1).start()

    def pass_near(m):
        for b in (LOW, HIGH) if m < comps - 1 else (LOW, OWN, HIGH):
            to_far(b, m).wait_recv()
            to_near(b, m, 1).start()

    def reduce_near(m):
        return remote(rs1_send.at[m], rs1_recv.at[m], rs1_sem.at[m], pair=near)

    def reduce_far(m):
        return remote(rs2_send.at[m], rs2_recv.at[m], rs2_sem.at[m], pair=far)

    def columns(index):
        return pl.ds(pl.multiple_of(index * q, q), q)

    def compute(m):
        for b in (LOW, OWN, HIGH):
            for which in range(2):
                to_near(b, m, which).wait_recv()
        window = jnp.concatenate(
            [jnp.concatenate([win[s, b, m] for s in range(pairs)], axis=1) for b in (LOW, OWN, HIGH)],
            axis=0,
        )
        for r in range(held):
            sign = 1 - 2 * (lax.shift_right_logical(p * held + r, m) & 1)
            summed = jnp.dot(cnt[r * boxes:(r + 1) * boxes, :], window, preferred_element_type=F32)
            mixed[:, r * coeffs:(r + 1) * coeffs] = (summed * sign.astype(F32)).astype(BF)
        part[m] = jnp.dot(
            mixed[...], op_v[...].reshape(held * coeffs, outs), preferred_element_type=F32
        )
        for h in range(half):
            rs1_send[m, h] = part[m, :, columns(2 * h + 1 - lo)].astype(BF)
        reduce_near(m).start()

    def fold(m):
        reduce_near(m).wait_recv()
        there = far // 2
        rs2_send[m] = (part[m, :, columns(far)] + rs1_recv[m, there].astype(F32)).astype(BF)
        reduce_far(m).start()

    def finish(m):
        reduce_far(m).wait_recv()
        total = part[m, :, columns(p)] + rs1_recv[m, hi].astype(F32) + rs2_recv[m].astype(F32)
        own_out[m] = total
        return total.astype(BF)

    def send_back(g, k, m):
        return remote(
            rt_send.at[m, g * slots:(g + 1) * slots], rt_recv.at[m, g * slots:(g + 1) * slots],
            rt_sem.at[g, m], cube=c - k,
        )

    def give_back(m, total):
        rt_send[m] = jnp.dot(pick_t[...], total, preferred_element_type=F32).astype(BF)
        for g, k in groups:
            @pl.when(inside(-k))
            def _(g=g, k=k):
                send_back(g, k, m).start()

    relay(0)
    to_far(OWN, comps - 1).start()
    count_part(2)
    relay(1)
    pass_near(0)
    count_part(3)
    relay(2)
    pass_near(1)
    count_part(4)
    for g, k in groups:
        pick_t[g * slots:(g + 1) * slots, :] = jnp.transpose(pick[g].astype(F32)).astype(BF)
    for r in range(held):
        for t in range(tiles):
            cnt[r * boxes:(r + 1) * boxes, t * LANES:(t + 1) * LANES] = cnt_f[
                pl.ds(r * tiles + t, boxes, stride=rows), :
            ].astype(BF)
    read_op.wait()
    compute(0)
    pass_near(2)
    compute(1)
    fold(0)
    compute(2)
    fold(1)
    give_back(0, finish(0))
    fold(2)
    give_back(1, finish(1))
    give_back(2, finish(2))

    for g, k in groups:
        rows_out = slice(g * slots, (g + 1) * slots)

        @pl.when(inside(k))
        def _(g=g, k=k, rows_out=rows_out):
            for m in range(comps):
                send_back(g, k, m).wait_recv()
                spill_out[m, rows_out, :] = rt_recv[m, rows_out, :].astype(F32)

        @pl.when(jnp.logical_not(inside(k)))
        def _(rows_out=rows_out):
            for m in range(comps):
                spill_out[m, rows_out, :] = jnp.zeros((slots, q), F32)

    for g, k in groups:
        @pl.when(inside(k))
        def _(g=g, k=k):
            for m in range(comps):
                send_spill(g, k, m).wait_send()
            send_label(g, k).wait_send()

        @pl.when(inside(-k))
        def _(g=g, k=k):
            for m in range(comps):
                send_back(g, k, m).wait_send()

    for m in range(comps):
        @pl.when(inside(1))
        def _(m=m):
            up(m).wait_send()

        @pl.when(inside(-1))
        def _(m=m):
            down(m).wait_send()

        for b in (LOW, OWN, HIGH):
            to_far(b, m).wait_send()
            to_near(b, m, 0).wait_send()
            to_near(b, m, 1).wait_send()
        reduce_near(m).wait_send()
        reduce_far(m).wait_send()


def on_device(cubes, pairs, own_partial, spill_partial, spill_box, sources, reflections, operators):
    comps, boxes, coeffs = own_partial.shape
    held, _, outs = operators.shape
    spills = spill_box.shape[0]
    groups = 2 * SPILL
    slots = spills // groups
    q = coeffs // pairs
    extent = 3 * boxes
    rows = -(-(held * extent // LANES) // 16) * 16
    width = -(-sources.shape[1] // LANES) * LANES
    dma = pltpu.SemaphoreType.DMA
    vmem = pl.BlockSpec(memory_space=pltpu.VMEM)
    anywhere = pl.BlockSpec(memory_space=pltpu.HBM)
    return pl.pallas_call(
        functools.partial(kernel, cubes, pairs),
        out_shape=(
            jax.ShapeDtypeStruct((comps, boxes, q), F32),
            jax.ShapeDtypeStruct((comps, spills, q), F32),
        ),
        in_specs=[anywhere] * 6,
        out_specs=(vmem, vmem),
        scratch_shapes=[
            pltpu.VMEM((comps, boxes, q), F32),
            pltpu.VMEM((comps, spills, q), F32),
            pltpu.VMEM((held, coeffs, outs), BF),
            pltpu.VMEM((1, spills), jnp.int32),
            pltpu.VMEM(sources.shape[::-1], jnp.int32),
            pltpu.VMEM(sources.shape[::-1], jnp.int32),
            pltpu.VMEM((groups, 8, LANES), jnp.int32),
            pltpu.VMEM((groups, 8, LANES), jnp.int32),
            pltpu.VMEM((groups, comps, slots, q), BF),
            pltpu.VMEM((groups, comps, slots, q), BF),
            pltpu.VMEM((width, boxes), F32),
            pltpu.VMEM((boxes, width), F32),
            pltpu.VMEM((boxes, width), F32),
            pltpu.VMEM((boxes * rows, LANES), F32),
            pltpu.VMEM((held * boxes, extent), BF),
            pltpu.VMEM((pairs, 3, comps, boxes, q), BF),
            pltpu.VMEM((boxes, held * coeffs), BF),
            pltpu.VMEM((comps, boxes, outs), F32),
            pltpu.VMEM((comps, pairs // 2, boxes, q), BF),
            pltpu.VMEM((comps, pairs // 2, boxes, q), BF),
            pltpu.VMEM((comps, boxes, q), BF),
            pltpu.VMEM((comps, boxes, q), BF),
            pltpu.VMEM((groups, boxes, slots), BF),
            pltpu.VMEM((spills, boxes), BF),
            pltpu.VMEM((comps, spills, q), BF),
            pltpu.VMEM((comps, spills, q), BF),
            dma((6,)),
            dma((groups, 2)),
            dma((groups, comps, 2)),
            dma((2, comps, 2)),
            dma((3, comps, 2)),
            dma((2, 3, comps, 2)),
            dma((comps, 2)),
            dma((comps, 2)),
            dma((groups, comps, 2)),
        ],
        compiler_params=pltpu.CompilerParams(
            collective_id=0, has_side_effects=True, vmem_limit_bytes=52 * 1024 * 1024
        ),
        name="far_field",
    )(own_partial, spill_partial, spill_box.reshape(1, spills), sources.T, reflections.T, operators)


def solution(mesh):
    cubes, pairs = mesh.shape["cube"], mesh.shape["pair"]
    in_specs = (
        P(None, "cube", None),
        P(None, "cube", None),
        P("cube"),
        P("cube", None),
        P("cube", None),
        P("pair", None, None),
    )
    out_specs = (P(None, "cube", "pair"), P(None, "cube", "pair"))
    return jax.shard_map(
        functools.partial(on_device, cubes, pairs),
        mesh=mesh, in_specs=in_specs, out_specs=out_specs, check_vma=False,
    )
```
